32 devices in a mesh: asset: 2 (over y), earn: 4 (over x, core), age: 4 (over z).
Axes of the slice: x: 2, y: 2, z: 4, core: 2. Of those that a mesh axis runs over, the one named last changes fastest.
Arguments:
- values: float32 [8, 32, 512, 512], P('age', 'earn', 'asset'), may hold values from -6 to 6
- utility: float32 [8, 32, 512, 512], P('age', 'earn', 'asset'), may hold values from -6 to 6
- earn_prob: float32 [5, 32], P(None, 'earn'), may hold values from 0.1 to 1
- support_start: int32 [32], P('earn'), may hold values from 0 to 27, as said below
- liquid_offset: int32 [32, 512], P('earn'), may hold values from 0 to 508
- liquid_weight: float32 [4, 32, 512], P(None, 'earn'), may hold values from 0.05 to 0.45
- illiquid_offset: int32 [32, 512], P('earn'), may hold values from 0 to 508
- illiquid_weight: float32 [4, 32, 512], P(None, 'earn'), may hold values from 0.05 to 0.45
Outputs:
- updated: float32 [8, 32, 512, 512], P('age', 'earn', 'asset')
The draws below stay inside these ranges and needn't reach their ends.
Inputs may be any that keep to these rules, and one draw needn't show every extreme that they name: support_start[e] lies between e - 4 and e, and support_start[e] + 4 is a valid state.
All inputs are finite; a program needn't handle non-finite values.
Results may differ from the reference program's by a relative error of at most 0.00005.
Values sent between devices are 32-bit elements; how exact they have to be, the bound alone decides.
A program may use at most 128 MiB of HBM per device.

```python
import math
import jax
import jax.numpy as jnp
from jax import lax

A = 512
B = 512
E = 32
REACH = 4
BAND = 4
ITERS = 2
AGES = 8


def draw_support_start(key, part):
    states = jnp.arange(E, dtype=jnp.int32)
    downward = jax.random.randint(key, (E,), 0, REACH + 1).astype(jnp.int32)
    phase = jax.random.randint(jax.random.fold_in(key, 7), (), 0, 4).astype(jnp.int32)
    downward = jnp.where(states % 4 == phase, REACH, downward)
    return jnp.clip(states - downward, 0, E - 1 - REACH).astype(jnp.int32)


def plant(values, own_key, smallest, largest):
    longest = values.shape.index(max(values.shape))
    spots = []
    for shift in (0, 1):
        where = [jax.random.randint(jax.random.fold_in(own_key, axis), (), 0, length) for axis, length in enumerate(values.shape)]
        where[longest] = (where[longest] + shift) % values.shape[longest]
        spots.append(tuple(where))
    return values.at[spots[0]].set(smallest).at[spots[1]].set(largest)


def levels(stream_key, extent, split, least, largest):
    gain = 1.0
    for axis_at, shards_of in split:
        draws = jax.random.uniform(jax.random.fold_in(jax.random.fold_in(stream_key, 6), axis_at), (shards_of,), jnp.float32, least / len(split), largest / len(split))
        gain = gain * jnp.repeat(jnp.exp(draws), extent[axis_at] // shards_of).reshape((-1,) + (1,) * (len(extent) - 1 - axis_at))
    return gain


def normal_values(stream_key, extent, width, limit, cuts=(), kind=jnp.bfloat16):
    level = levels(stream_key, extent, cuts, -0.22, 0.18) if cuts else 1.0
    array = jax.random.normal(stream_key, extent, jnp.float32) * width * level
    return jnp.minimum(jnp.maximum(array, -limit), limit).astype(kind)


def setup_inputs(seed: int = 0) -> dict:
    seeds = jax.random.split(jax.random.key(seed), 9)
    return {
        "values": normal_values(seeds[0], (AGES, E, B, A), 1.0, 6.0, ((0, 4), (1, 4), (2, 2)), jnp.float32),
        "utility": normal_values(seeds[1], (AGES, E, B, A), 1.0, 6.0, ((0, 4), (1, 4), (2, 2)), jnp.float32),
        "earn_prob": jnp.clip(jnp.exp(math.log(1.0) - 2.3025851 * jax.random.uniform(seeds[2], (REACH + 1, E), jnp.float32) ** levels(seeds[2], (REACH + 1, E), ((1, 4),), -0.2, 0.2)), 0.1, 1.0),
        "support_start": draw_support_start(jax.random.fold_in(seeds[8], 71), 0),
        "liquid_offset": plant(jax.random.randint(seeds[4], (E, A), 0, A - BAND + 1), jax.random.fold_in(seeds[4], 1), 0, A - BAND).astype(jnp.int32),
        "liquid_weight": jnp.clip(0.05 + 0.39999999 * jax.random.uniform(seeds[5], (BAND, E, A), jnp.float32) ** levels(seeds[5], (BAND, E, A), ((1, 4),), -0.2, 0.2), 0.05, 0.45),
        "illiquid_offset": plant(jax.random.randint(seeds[6], (E, B), 0, B - BAND + 1), jax.random.fold_in(seeds[6], 1), 0, B - BAND).astype(jnp.int32),
        "illiquid_weight": jnp.clip(0.05 + 0.39999999 * jax.random.uniform(seeds[7], (BAND, E, B), jnp.float32) ** levels(seeds[7], (BAND, E, B), ((1, 4),), -0.2, 0.2), 0.05, 0.45),
    }


DISCOUNT = 0.96


def liquid_one(pieces):
    stacked, offset, weight = pieces
    result = jnp.zeros_like(stacked)
    for number in range(BAND):
        result = result + weight[number][None, None, :] * stacked[:, :, offset + number]
    return result


def illiquid_one(pieces):
    stacked, offset, weight = pieces
    result = jnp.zeros_like(stacked)
    for number in range(BAND):
        result = result + weight[number][None, :, None] * stacked[:, offset + number, :]
    return result


def reference(values, utility, earn_prob, support_start, liquid_offset, liquid_weight, illiquid_offset, illiquid_weight):
    shares = earn_prob / jnp.sum(earn_prob, axis=0, keepdims=True)
    current = values
    for iteration in range(ITERS):
        following = jnp.concatenate([current[1:], jnp.zeros_like(current[:1])], axis=0)
        expected = jnp.zeros_like(current)
        for number in range(REACH + 1):
            expected = expected + shares[number][None, :, None, None] * following[:, support_start + number]
        moved = jnp.moveaxis(expected, 1, 0)
        saved = lax.map(liquid_one, (moved, liquid_offset, jnp.moveaxis(liquid_weight, 1, 0)))
        adjusted = lax.map(illiquid_one, (saved, illiquid_offset, jnp.moveaxis(illiquid_weight, 1, 0)))
        current = utility + DISCOUNT * jnp.moveaxis(adjusted, 0, 1)
    return current
```

```python
import functools

import jax
import jax.numpy as jnp
from jax import lax
from jax.experimental import pallas as pl
from jax.experimental.pallas import tpu as pltpu
from jax.sharding import PartitionSpec as P

REACH = 4
BAND = 4
DISCOUNT = 0.96
SPAN = 2 * REACH + 1
VMEM_BYTES = 48 * 1024 * 1024


def params():
    return pltpu.CompilerParams(vmem_limit_bytes=VMEM_BYTES)


def halves(x):
    high = x.astype(jnp.bfloat16)
    return high, (x - high.astype(jnp.float32)).astype(jnp.bfloat16)


def dot3(ah, al, bh, bl):
    dot = functools.partial(jnp.dot, preferred_element_type=jnp.float32)
    return dot(ah, bh) + (dot(ah, bl) + dot(al, bh))


def band_kernel(flip, bases, offset, weight, high, low, full):
    count = bases.shape[0]
    extent = full.shape[0]
    width = extent // count
    step = min(width, 32)
    first = offset[0]
    for block in range(count):
        for row in range(0, width, step):
            place = lax.broadcasted_iota(jnp.int32, (step, extent), 0) + (bases[block] + row)
            gap = place - first
            value = jnp.zeros((step, extent), jnp.float32)
            for number in range(BAND):
                value = jnp.where(gap == number, weight[number, 0], value)
            full[pl.ds(block * width + row, step), :] = value
    matrix = full[...]
    if flip:
        matrix = matrix.T
    high[0], low[0] = halves(matrix)


def band_pair(offset, weight, bases, flip):
    states, extent = offset.shape
    out = jax.ShapeDtypeStruct((states, extent, extent), jnp.bfloat16)
    spec = pl.BlockSpec((1, extent, extent), lambda e: (e, 0, 0))
    return pl.pallas_call(
        functools.partial(band_kernel, flip),
        grid=(states,),
        out_shape=(out, out),
        in_specs=[
            pl.BlockSpec(memory_space=pltpu.SMEM),
            pl.BlockSpec((1, 1, extent), lambda e: (e, 0, 0)),
            pl.BlockSpec((BAND, 1, 1, extent), lambda e: (0, e, 0, 0)),
        ],
        out_specs=(spec, spec),
        scratch_shapes=[pltpu.VMEM((extent, extent), jnp.float32)],
        compiler_params=params(),
        cost_estimate=pl.CostEstimate(
            flops=states * extent * extent * 12, bytes_accessed=states * extent * extent * 4, transcendentals=0
        ),
        name="band",
    )(bases, offset[:, None, :], weight[:, :, None, :])


def mix_kernel(base, left_product, pieces, mixing, below, here, above, high, low, *rest):
    outs, (slabs, xh, xl, sems) = rest[:pieces], rest[pieces:]
    e = pl.program_id(0)
    quad = here.shape[0]

    def fetch(source, group):
        return [
            pltpu.make_async_copy(source.at[i], slabs.at[group * quad + i], sems.at[group * quad + i])
            for i in range(quad)
        ]

    copies = fetch(below, 0) + fetch(here, 1) + fetch(above, 2)

    @pl.when(e == 0)
    def _():
        for copy in copies:
            copy.start()
        for copy in copies[: SPAN - 1]:
            copy.wait()

    for number in range(quad):

        @pl.when(e == number)
        def _():
            copies[number + SPAN - 1].wait()

    rows = xh.shape[0]
    step = 16
    shares = [mixing[base + e, d] for d in range(SPAN)]

    def chunk(i, carry):
        at = pl.ds(pl.multiple_of(i * step, step), step)
        total = shares[0] * slabs[e, at, :]
        for d in range(1, SPAN):
            total = total + shares[d] * slabs[e + d, at, :]
        xh[at, :], xl[at, :] = halves(total)
        return carry

    lax.fori_loop(0, rows // step, chunk, 0)
    if left_product:
        result = dot3(high[0], low[0], xh[...], xl[...])
        width = result.shape[0] // pieces
        for s in range(pieces):
            outs[s][0] = result[s * width : (s + 1) * width]
    else:
        result = dot3(xh[...], xl[...], high[0], low[0])
        width = result.shape[1] // pieces
        for s in range(pieces):
            outs[s][0] = result[:, s * width : (s + 1) * width]


def mixed_product(below, here, above, mixing, pair, base, left_product, pieces):
    quad, rows, columns = here.shape
    extent = pair[0].shape[1]
    shape = (rows // pieces, columns) if left_product else (rows, columns // pieces)
    matrix = pl.BlockSpec((1, extent, extent), lambda e: (base + e, 0, 0))
    return pl.pallas_call(
        functools.partial(mix_kernel, base, left_product, pieces),
        grid=(quad,),
        out_shape=[jax.ShapeDtypeStruct((quad,) + shape, jnp.float32)] * pieces,
        in_specs=[pl.BlockSpec(memory_space=pltpu.SMEM)]
        + [pl.BlockSpec(memory_space=pl.ANY)] * 3
        + [matrix] * 2,
        out_specs=[pl.BlockSpec((1,) + shape, lambda e: (e, 0, 0))] * pieces,
        scratch_shapes=[
            pltpu.VMEM((3 * quad, rows, columns), jnp.float32),
            pltpu.VMEM((rows, columns), jnp.bfloat16),
            pltpu.VMEM((rows, columns), jnp.bfloat16),
            pltpu.SemaphoreType.DMA((3 * quad,)),
        ],
        compiler_params=params(),
        cost_estimate=pl.CostEstimate(
            flops=quad * rows * columns * extent * 6,
            bytes_accessed=4 * quad * rows * columns * 4 + 4 * quad * extent * extent,
            transcendentals=0,
        ),
        name="mix_band",
    )(mixing, below, here, above, *pair)


def column_kernel(pieces, high, low, *rest):
    parts, flows, (out, xh, xl) = rest[:pieces], rest[pieces : 2 * pieces], rest[2 * pieces :]
    rows = parts[0].shape[1]
    for s in range(pieces):
        at = pl.ds(s * rows, rows)
        xh[at, :], xl[at, :] = halves(parts[s][0])
    result = dot3(high[0], low[0], xh[...], xl[...])
    for s in range(pieces):
        at = pl.ds(s * rows, rows)
        out[0, at, :] = flows[s][0] + DISCOUNT * result[s * rows : (s + 1) * rows]


def column_product(parts, flows, pair, base):
    pieces = len(parts)
    quad, rows, columns = parts[0].shape
    extent = pair[0].shape[1]
    matrix = pl.BlockSpec((1, extent, extent), lambda e: (base + e, 0, 0))
    piece = pl.BlockSpec((1, rows, columns), lambda e: (e, 0, 0))
    flow = pl.BlockSpec((1, rows, columns), lambda e: (base + e, 0, 0))
    return pl.pallas_call(
        functools.partial(column_kernel, pieces),
        grid=(quad,),
        out_shape=jax.ShapeDtypeStruct((quad, extent, columns), jnp.float32),
        in_specs=[matrix] * 2 + [piece] * pieces + [flow] * pieces,
        out_specs=pl.BlockSpec((1, extent, columns), lambda e: (e, 0, 0)),
        scratch_shapes=[pltpu.VMEM((extent, columns), jnp.bfloat16)] * 2,
        compiler_params=params(),
        cost_estimate=pl.CostEstimate(
            flops=quad * extent * columns * extent * 6,
            bytes_accessed=3 * quad * extent * columns * 4 + 4 * quad * extent * extent,
            transcendentals=0,
        ),
        name="columns_band",
    )(*pair, *parts, *flows)


def row_product_of(parts, high, low):
    width = parts[0].shape[2]
    result = None
    for s, part in enumerate(parts):
        xh, xl = halves(part[0])
        at = pl.ds(s * width, width)
        term = dot3(xh, xl, high[0, at, :], low[0, at, :])
        result = term if result is None else result + term
    return result


def row_kernel(pieces, high, low, *rest):
    parts, out = rest[:pieces], rest[pieces]
    out[0] = row_product_of(parts, high, low)


def row_product(parts, pair, base):
    pieces = len(parts)
    quad, rows, columns = parts[0].shape
    extent = pair[0].shape[1]
    matrix = pl.BlockSpec((1, extent, extent), lambda e: (base + e, 0, 0))
    piece = pl.BlockSpec((1, rows, columns), lambda e: (e, 0, 0))
    return pl.pallas_call(
        functools.partial(row_kernel, pieces),
        grid=(quad,),
        out_shape=jax.ShapeDtypeStruct((quad, rows, extent), jnp.float32),
        in_specs=[matrix] * 2 + [piece] * pieces,
        out_specs=pl.BlockSpec((1, rows, extent), lambda e: (e, 0, 0)),
        compiler_params=params(),
        cost_estimate=pl.CostEstimate(
            flops=quad * rows * extent * extent * 6,
            bytes_accessed=2 * quad * rows * extent * 4 + 4 * quad * extent * extent,
            transcendentals=0,
        ),
        name="rows_band",
    )(*pair, *parts)


def last_row_kernel(pieces, high, low, flow, *rest):
    parts, out = rest[:pieces], rest[-1]
    out[0, 0] = flow[0, 0] + DISCOUNT * row_product_of(parts, high, low)


def last_rows(parts, pair, base, utility, age, whole):
    pieces = len(parts)
    quad, rows, columns = parts[0].shape
    extent = pair[0].shape[1]
    matrix = pl.BlockSpec((1, extent, extent), lambda e: (base + e, 0, 0))
    piece = pl.BlockSpec((1, rows, columns), lambda e: (e, 0, 0))
    flow = pl.BlockSpec((1, 1, rows, extent), lambda e: (age, base + e, 0, 0))
    return pl.pallas_call(
        functools.partial(last_row_kernel, pieces),
        grid=(quad,),
        out_shape=jax.ShapeDtypeStruct(utility.shape, jnp.float32),
        in_specs=[matrix] * 2 + [flow] + [piece] * pieces + [pl.BlockSpec(memory_space=pl.ANY)],
        out_specs=flow,
        input_output_aliases={3 + pieces: 0},
        compiler_params=params(),
        cost_estimate=pl.CostEstimate(
            flops=quad * rows * extent * extent * 6,
            bytes_accessed=3 * quad * rows * extent * 4 + 4 * quad * extent * extent,
            transcendentals=0,
        ),
        name="last_rows",
    )(*pair, utility, *parts, whole)


def add_kernel(flow, arrived, *rest):
    rest[-1][0, 0] = flow[0, 0] + DISCOUNT * arrived[0]


def last_sum(arrived, base, utility, age, whole):
    quad, rows, extent = arrived.shape
    flow = pl.BlockSpec((1, 1, rows, extent), lambda e: (age, base + e, 0, 0))
    part = pl.BlockSpec((1, rows, extent), lambda e: (e, 0, 0))
    before = () if whole is None else (whole,)
    return pl.pallas_call(
        add_kernel,
        grid=(quad,),
        out_shape=jax.ShapeDtypeStruct(utility.shape, jnp.float32),
        in_specs=[flow, part] + [pl.BlockSpec(memory_space=pl.ANY)] * len(before),
        out_specs=flow,
        input_output_aliases={} if whole is None else {2: 0},
        compiler_params=params(),
        cost_estimate=pl.CostEstimate(
            flops=quad * rows * extent * 2, bytes_accessed=3 * quad * rows * extent * 4, transcendentals=0
        ),
        name="last_sum",
    )(utility, arrived, *before)


def shifted(value, axis, by):
    count = lax.axis_size(axis)
    return lax.ppermute(value, axis, [(i, i + by) for i in range(count) if 0 <= i + by < count])


def exchanged(pieces):
    count = lax.axis_size("asset")
    return [pieces[0]] + [
        lax.ppermute(pieces[s], "asset", [(i, (i + s) % count) for i in range(count)])
        for s in range(1, count)
    ]


def local(
    values,
    utility,
    earn_prob,
    support_start,
    liquid_offset,
    liquid_weight,
    illiquid_offset,
    illiquid_weight,
):
    count = lax.axis_size("asset")
    me = lax.axis_index("asset")
    states = values.shape[1]
    quad = REACH
    assert states == 2 * quad
    rows = values.shape[2]
    columns = values.shape[3] // count

    ahead = [(me + s) % count for s in range(count)]
    behind = [(me - s + count) % count for s in range(count)]

    def in_blocks(x, blocks, width):
        return jnp.concatenate(
            [lax.dynamic_slice_in_dim(x, block * width, width, axis=x.ndim - 1) for block in blocks], axis=-1
        )

    def starts(blocks, width):
        return jnp.stack([jnp.asarray(block * width, jnp.int32) for block in blocks])

    natural_columns = starts(range(count), columns)
    behind_columns = starts(behind, columns)
    behind_rows = starts(behind, rows)

    liquid_first = band_pair(
        in_blocks(liquid_offset, ahead, columns), in_blocks(liquid_weight, ahead, columns), natural_columns, False
    )
    illiquid_first = band_pair(
        in_blocks(illiquid_offset, behind, rows), in_blocks(illiquid_weight, behind, rows), behind_rows, True
    )
    if count == 2:
        illiquid_second = illiquid_first
    else:
        illiquid_second = band_pair(
            in_blocks(illiquid_offset, ahead, rows), in_blocks(illiquid_weight, ahead, rows), behind_rows, True
        )
    liquid_second = band_pair(liquid_offset, liquid_weight, behind_columns, False)

    shares = earn_prob / jnp.sum(earn_prob, axis=0, keepdims=True)
    own = lax.axis_index("earn") * states + jnp.arange(states, dtype=jnp.int32)
    slots = jnp.arange(SPAN, dtype=jnp.int32)
    mixing = jnp.zeros((states, SPAN), jnp.float32)
    for number in range(REACH + 1):
        slot = support_start + number - own + REACH
        mixing = mixing + jnp.where(slots[None, :] == slot[:, None], shares[number][:, None], 0.0)

    def with_sides(head, tail):
        return [shifted(tail, "earn", 1), head, tail, shifted(head, "earn", -1)]

    def first_half(head, tail):
        quads = with_sides(head, tail)
        return [
            exchanged(mixed_product(*quads[i : i + 3], mixing, liquid_first, i * quad, False, count))
            for i in range(2)
        ]

    def middle(arrived, flows):
        return [column_product(arrived[i], flows, illiquid_first, i * quad) for i in range(2)]

    def second_half(head, tail):
        quads = with_sides(head, tail)
        return [
            exchanged(mixed_product(*quads[i : i + 3], mixing, illiquid_second, i * quad, True, count))
            for i in range(2)
        ]

    def flow_columns(age):
        return exchanged(
            [lax.dynamic_slice_in_dim(utility[age], block * columns, columns, axis=2) for block in ahead]
        )

    coming = [shifted(values[0, i * quad : (i + 1) * quad], "age", -1) for i in range(2)]

    flows = flow_columns(0)
    arrived = first_half(values[1, :quad], values[1, quad:])
    arrived = second_half(*middle(arrived, flows))
    passed = [shifted(row_product(arrived[i], liquid_second, i * quad), "age", -1) for i in range(2)]

    flows = flow_columns(1)
    arrived = first_half(*coming)
    arrived = second_half(*middle(arrived, flows))

    whole = None
    for i in range(2):
        whole = last_sum(passed[i], i * quad, utility, 1, whole)
    for i in range(2):
        whole = last_rows(arrived[i], liquid_second, i * quad, utility, 0, whole)
    return whole


def solution(mesh):
    return jax.shard_map(
        local,
        mesh=mesh,
        in_specs=(
            P("age", "earn", "asset", None),
            P("age", "earn", "asset", None),
            P(None, "earn"),
            P("earn"),
            P("earn", None),
            P(None, "earn", None),
            P("earn", None),
            P(None, "earn", None),
        ),
        out_specs=P("age", "earn", "asset", None),
        check_vma=False,
    )
```

```python
import functools

import jax
import jax.numpy as jnp
from jax import lax
from jax.experimental import pallas as pl
from jax.experimental.pallas import tpu as pltpu
from jax.sharding import PartitionSpec as P

REACH = 4
BAND = 4
DISCOUNT = 0.96
SPAN = 2 * REACH + 1
VMEM_BYTES = 60 * 1024 * 1024


def params():
    return pltpu.CompilerParams(vmem_limit_bytes=VMEM_BYTES)


def ordered_call(kernel, after, in_specs, **rest):
    known, extra = len(in_specs), len(after)

    def body(*refs):
        kernel(*refs[:known], *refs[known + extra :])

    call = pl.pallas_call(
        body,
        in_specs=list(in_specs) + [pl.BlockSpec(memory_space=pl.ANY)] * extra,
        compiler_params=params(),
        **rest,
    )
    return lambda *operands: call(*operands, *after)


def halves(x):
    high = x.astype(jnp.bfloat16)
    return high, (x - high.astype(jnp.float32)).astype(jnp.bfloat16)


def dot3(ah, al, bh, bl):
    dot = functools.partial(jnp.dot, preferred_element_type=jnp.float32)
    return dot(ah, bh) + (dot(ah, bl) + dot(al, bh))


def band_kernel(flip, bases, offset, weight, high, low, full):
    count = bases.shape[0]
    extent = full.shape[0]
    width = extent // count
    step = min(width, 32)
    first = offset[0]
    for block in range(count):
        for row in range(0, width, step):
            place = lax.broadcasted_iota(jnp.int32, (step, extent), 0) + (bases[block] + row)
            gap = place - first
            value = jnp.zeros((step, extent), jnp.float32)
            for number in range(BAND):
                value = jnp.where(gap == number, weight[number, 0], value)
            full[pl.ds(block * width + row, step), :] = value
    matrix = full[...]
    if flip:
        matrix = matrix.T
    high[0], low[0] = halves(matrix)


def band_pair(offset, weight, bases, flip):
    states, extent = offset.shape
    out = jax.ShapeDtypeStruct((states, extent, extent), jnp.bfloat16)
    spec = pl.BlockSpec((1, extent, extent), lambda e: (e, 0, 0))
    return pl.pallas_call(
        functools.partial(band_kernel, flip),
        grid=(states,),
        out_shape=(out, out),
        in_specs=[
            pl.BlockSpec(memory_space=pltpu.SMEM),
            pl.BlockSpec((1, 1, extent), lambda e: (e, 0, 0)),
            pl.BlockSpec((BAND, 1, 1, extent), lambda e: (0, e, 0, 0)),
        ],
        out_specs=(spec, spec),
        scratch_shapes=[pltpu.VMEM((extent, extent), jnp.float32)],
        compiler_params=params(),
        cost_estimate=pl.CostEstimate(
            flops=states * extent * extent * 12, bytes_accessed=states * extent * extent * 4, transcendentals=0
        ),
        name="band",
    )(bases, offset[:, None, :], weight[:, :, None, :])


def mix_kernel(base, left_product, pieces, places, mixing, below, here, above, high, low, *rest):
    outs, (slabs, xh, xl, sems) = rest[:pieces], rest[pieces:]
    e = pl.program_id(0)
    quad = slabs.shape[0] // 3

    def fetch(source, group):
        place = places[group]
        return [
            pltpu.make_async_copy(source.at[i] if place is None else source.at[place[0], place[1] + i], slabs.at[group * quad + i], sems.at[group * quad + i])
            for i in range(quad)
        ]

    copies = fetch(below, 0) + fetch(here, 1) + fetch(above, 2)

    @pl.when(e == 0)
    def _():
        for copy in copies:
            copy.start()
        for copy in copies[: SPAN - 1]:
            copy.wait()

    for number in range(quad):

        @pl.when(e == number)
        def _():
            copies[number + SPAN - 1].wait()

    rows = xh.shape[0]
    step = 16
    shares = [mixing[base + e, d] for d in range(SPAN)]

    def chunk(i, carry):
        at = pl.ds(pl.multiple_of(i * step, step), step)
        total = shares[0] * slabs[e, at, :]
        for d in range(1, SPAN):
            total = total + shares[d] * slabs[e + d, at, :]
        xh[at, :], xl[at, :] = halves(total)
        return carry

    lax.fori_loop(0, rows // step, chunk, 0)
    if left_product:
        result = dot3(high[0], low[0], xh[...], xl[...])
        width = result.shape[0] // pieces
        for s in range(pieces):
            outs[s][0] = result[s * width : (s + 1) * width]
    else:
        result = dot3(xh[...], xl[...], high[0], low[0])
        width = result.shape[1] // pieces
        for s in range(pieces):
            outs[s][0] = result[:, s * width : (s + 1) * width]


def mixed_product(sources, mixing, pair, base, left_product, pieces, after=()):
    quad = REACH
    arrays = [source[0] if isinstance(source, tuple) else source for source in sources]
    places = [source[1:] if isinstance(source, tuple) else None for source in sources]
    rows, columns = arrays[0].shape[-2:]
    extent = pair[0].shape[1]
    shape = (rows // pieces, columns) if left_product else (rows, columns // pieces)
    matrix = pl.BlockSpec((1, extent, extent), lambda e: (base + e, 0, 0))
    return ordered_call(
        functools.partial(mix_kernel, base, left_product, pieces, places),
        after,
        grid=(quad,),
        out_shape=[jax.ShapeDtypeStruct((quad,) + shape, jnp.float32)] * pieces,
        in_specs=[pl.BlockSpec(memory_space=pltpu.SMEM)]
        + [pl.BlockSpec(memory_space=pl.ANY)] * 3
        + [matrix] * 2,
        out_specs=[pl.BlockSpec((1,) + shape, lambda e: (e, 0, 0))] * pieces,
        scratch_shapes=[
            pltpu.VMEM((3 * quad, rows, columns), jnp.float32),
            pltpu.VMEM((rows, columns), jnp.bfloat16),
            pltpu.VMEM((rows, columns), jnp.bfloat16),
            pltpu.SemaphoreType.DMA((3 * quad,)),
        ],
        cost_estimate=pl.CostEstimate(
            flops=quad * rows * columns * extent * 6,
            bytes_accessed=4 * quad * rows * columns * 4 + 4 * quad * extent * extent,
            transcendentals=0,
        ),
        name="mix_band",
    )(mixing, *arrays, *pair)


def column_kernel(pieces, high, low, *rest):
    parts, flows, (out, xh, xl) = rest[:pieces], rest[pieces : 2 * pieces], rest[2 * pieces :]
    rows = parts[0].shape[1]
    for s in range(pieces):
        at = pl.ds(s * rows, rows)
        xh[at, :], xl[at, :] = halves(parts[s][0])
    result = dot3(high[0], low[0], xh[...], xl[...])
    for s in range(pieces):
        at = pl.ds(s * rows, rows)
        out[0, at, :] = flows[s][0] + DISCOUNT * result[s * rows : (s + 1) * rows]


def column_product(parts, flows, pair, base, after=()):
    pieces = len(parts)
    quad, rows, columns = parts[0].shape
    extent = pair[0].shape[1]
    matrix = pl.BlockSpec((1, extent, extent), lambda e: (base + e, 0, 0))
    piece = pl.BlockSpec((1, rows, columns), lambda e: (e, 0, 0))
    return ordered_call(
        functools.partial(column_kernel, pieces),
        after,
        grid=(quad,),
        out_shape=jax.ShapeDtypeStruct((quad, extent, columns), jnp.float32),
        in_specs=[matrix] * 2 + [piece] * (2 * pieces),
        out_specs=pl.BlockSpec((1, extent, columns), lambda e: (e, 0, 0)),
        scratch_shapes=[pltpu.VMEM((extent, columns), jnp.bfloat16)] * 2,
        cost_estimate=pl.CostEstimate(
            flops=quad * extent * columns * extent * 6,
            bytes_accessed=3 * quad * extent * columns * 4 + 4 * quad * extent * extent,
            transcendentals=0,
        ),
        name="columns_band",
    )(*pair, *parts, *flows)


def row_product_of(parts, high, low):
    width = parts[0].shape[2]
    result = None
    for s, part in enumerate(parts):
        xh, xl = halves(part[0])
        at = pl.ds(s * width, width)
        term = dot3(xh, xl, high[0, at, :], low[0, at, :])
        result = term if result is None else result + term
    return result


def last_row_kernel(pieces, high, low, flow, *rest):
    parts, out = rest[:pieces], rest[-1]
    out[0, 0] = flow[0, 0] + DISCOUNT * row_product_of(parts, high, low)


def last_rows(parts, pair, base, utility, age, whole, after=()):
    pieces = len(parts)
    quad, rows, columns = parts[0].shape
    extent = pair[0].shape[1]
    matrix = pl.BlockSpec((1, extent, extent), lambda e: (base + e, 0, 0))
    piece = pl.BlockSpec((1, rows, columns), lambda e: (e, 0, 0))
    flow = pl.BlockSpec((1, 1, rows, extent), lambda e: (age, base + e, 0, 0))
    before = () if whole is None else (whole,)
    return ordered_call(
        functools.partial(last_row_kernel, pieces),
        after,
        grid=(quad,),
        out_shape=jax.ShapeDtypeStruct(utility.shape, jnp.float32),
        in_specs=[matrix] * 2 + [flow] + [piece] * pieces + [pl.BlockSpec(memory_space=pl.ANY)] * len(before),
        out_specs=flow,
        input_output_aliases={} if whole is None else {3 + pieces: 0},
        cost_estimate=pl.CostEstimate(
            flops=quad * rows * extent * extent * 6,
            bytes_accessed=3 * quad * rows * extent * 4 + 4 * quad * extent * extent,
            transcendentals=0,
        ),
        name="last_rows",
    )(*pair, utility, *parts, *before)


def take_kernel(place, flow, out):
    out[0] = flow[0, 0]


def taken_columns(utility, age, base, block, columns, after=()):
    quad = REACH
    rows = utility.shape[2]
    if columns % 128:
        return lax.dynamic_slice_in_dim(utility[age, base : base + quad], block * columns, columns, axis=2)
    return pl.pallas_call(
        lambda place, flow, *rest: take_kernel(place, flow, rest[-1]),
        out_shape=jax.ShapeDtypeStruct((quad, rows, columns), jnp.float32),
        grid_spec=pltpu.PrefetchScalarGridSpec(
            num_scalar_prefetch=1,
            grid=(quad,),
            in_specs=[pl.BlockSpec((1, 1, rows, columns), lambda e, place: (age, base + e, 0, place[0]))]
            + [pl.BlockSpec(memory_space=pl.ANY)] * len(after),
            out_specs=pl.BlockSpec((1, rows, columns), lambda e, place: (e, 0, 0)),
        ),
        compiler_params=params(),
        cost_estimate=pl.CostEstimate(
            flops=0, bytes_accessed=2 * quad * rows * columns * 4, transcendentals=0
        ),
        name="take",
    )(jnp.reshape(jnp.asarray(block, jnp.int32), (1,)), utility, *after)


def shifted(value, axis, by):
    count = lax.axis_size(axis)
    return lax.ppermute(value, axis, [(i, i + by) for i in range(count) if 0 <= i + by < count])


def exchanged(pieces, by=0):
    count, ages = lax.axis_size("asset"), lax.axis_size("age")
    return [
        piece
        if s == 0 and by == 0
        else lax.ppermute(
            piece,
            ("asset", "age"),
            [
                (a * ages + z, (a + s) % count * ages + z + by)
                for a in range(count)
                for z in range(ages)
                if 0 <= z + by < ages
            ],
        )
        for s, piece in enumerate(pieces)
    ]


def local(
    values,
    utility,
    earn_prob,
    support_start,
    liquid_offset,
    liquid_weight,
    illiquid_offset,
    illiquid_weight,
):
    count = lax.axis_size("asset")
    me = lax.axis_index("asset")
    states = values.shape[1]
    quad = REACH
    assert states == 2 * quad
    rows = values.shape[2]
    columns = values.shape[3] // count

    ahead = [(me + s) % count for s in range(count)]
    behind = [(me - s + count) % count for s in range(count)]

    def in_blocks(x, blocks, width):
        return jnp.concatenate(
            [lax.dynamic_slice_in_dim(x, block * width, width, axis=x.ndim - 1) for block in blocks], axis=-1
        )

    def starts(blocks, width):
        return jnp.stack([jnp.asarray(block * width, jnp.int32) for block in blocks])

    natural_columns = starts(range(count), columns)
    behind_columns = starts(behind, columns)
    behind_rows = starts(behind, rows)

    liquid_first = band_pair(
        in_blocks(liquid_offset, ahead, columns), in_blocks(liquid_weight, ahead, columns), natural_columns, False
    )
    illiquid_first = band_pair(
        in_blocks(illiquid_offset, behind, rows), in_blocks(illiquid_weight, behind, rows), behind_rows, True
    )
    if count == 2:
        illiquid_second = illiquid_first
    else:
        illiquid_second = band_pair(
            in_blocks(illiquid_offset, ahead, rows), in_blocks(illiquid_weight, ahead, rows), behind_rows, True
        )
    liquid_second = band_pair(liquid_offset, liquid_weight, behind_columns, False)

    shares = earn_prob / jnp.sum(earn_prob, axis=0, keepdims=True)
    own = lax.axis_index("earn") * states + jnp.arange(states, dtype=jnp.int32)
    slots = jnp.arange(SPAN, dtype=jnp.int32)
    mixing = jnp.zeros((states, SPAN), jnp.float32)
    for number in range(REACH + 1):
        slot = support_start + number - own + REACH
        mixing = mixing + jnp.where(slots[None, :] == slot[:, None], shares[number][:, None], 0.0)

    def first_half(age, by, after):
        left = shifted(values[age, quad:], "earn", 1)
        right = shifted(values[age, :quad], "earn", -1)
        head, tail = (values, age, 0), (values, age, quad)
        parts = [mixed_product((left, head, tail), mixing, liquid_first, 0, False, count, after)]
        parts.append(mixed_product((head, tail, right), mixing, liquid_first, quad, False, count, (parts[0][0],)))
        return parts[1][0], [exchanged(part, by) for part in parts]

    def flow_columns(age, i, after):
        parts = [taken_columns(utility, age, i * quad, block, columns, after) for block in ahead]
        return parts[0], exchanged(parts)

    def middle(arrived, flows, i, after):
        return column_product(arrived[i], flows[i], illiquid_first, i * quad, after)

    def second_half(sides, i, after):
        return mixed_product(sides, mixing, illiquid_second, i * quad, True, count, after)

    done, flow_a = zip(*[flow_columns(0, i, ()) for i in range(2)])
    done, arrived_a = first_half(1, 0, tuple(done))
    done, arrived_b = first_half(0, -1, (done,))

    head_a = middle(arrived_a, flow_a, 0, (done,))
    right_a = shifted(head_a, "earn", -1)
    tail_a = middle(arrived_a, flow_a, 1, (head_a,))
    left_a = shifted(tail_a, "earn", 1)
    first, flow_b0 = flow_columns(1, 0, (tail_a,))
    second, flow_b1 = flow_columns(1, 1, (first,))
    flow_b = (flow_b0, flow_b1)

    parts = second_half((head_a, tail_a, right_a), 1, (second,))
    last_a1 = exchanged(parts, -1)
    head_b = middle(arrived_b, flow_b, 0, (parts[0],))
    right_b = shifted(head_b, "earn", -1)
    parts = second_half((left_a, head_a, tail_a), 0, (head_b,))
    last_a0 = exchanged(parts, -1)
    tail_b = middle(arrived_b, flow_b, 1, (parts[0],))
    left_b = shifted(tail_b, "earn", 1)

    parts = second_half((head_b, tail_b, right_b), 1, (tail_b,))
    last_b1 = exchanged(parts)
    parts = second_half((left_b, head_b, tail_b), 0, (parts[0],))
    last_b0 = exchanged(parts)

    whole = last_rows(last_a1, liquid_second, quad, utility, 1, None, (parts[0],))
    whole = last_rows(last_a0, liquid_second, 0, utility, 1, whole)
    whole = last_rows(last_b1, liquid_second, quad, utility, 0, whole)
    return last_rows(last_b0, liquid_second, 0, utility, 0, whole)


def solution(mesh):
    return jax.shard_map(
        local,
        mesh=mesh,
        in_specs=(
            P("age", "earn", "asset", None),
            P("age", "earn", "asset", None),
            P(None, "earn"),
            P("earn"),
            P("earn", None),
            P(None, "earn", None),
            P("earn", None),
            P(None, "earn", None),
        ),
        out_specs=P("age", "earn", "asset", None),
        check_vma=False,
    )
```

```python
import functools

import jax
import jax.numpy as jnp
from jax import lax
from jax.experimental import pallas as pl
from jax.experimental.pallas import tpu as pltpu
from jax.sharding import PartitionSpec as P

REACH = 4
BAND = 4
DISCOUNT = 0.96
SPAN = 2 * REACH + 1
VMEM_BYTES = 60 * 1024 * 1024
HINT = pl.CostEstimate(flops=1024, bytes_accessed=1024, transcendentals=0)


def params():
    return pltpu.CompilerParams(vmem_limit_bytes=VMEM_BYTES)


def ordered_call(kernel, after, in_specs, **rest):
    known, extra = len(in_specs), len(after)

    def body(*refs):
        kernel(*refs[:known], *refs[known + extra :])

    call = pl.pallas_call(
        body,
        in_specs=list(in_specs) + [pl.BlockSpec(memory_space=pl.ANY)] * extra,
        compiler_params=params(),
        **rest,
    )
    return lambda *operands: call(*operands, *after)


def halves(x):
    high = x.astype(jnp.bfloat16)
    return high, (x - high.astype(jnp.float32)).astype(jnp.bfloat16)


def dot3(ah, al, bh, bl):
    dot = functools.partial(jnp.dot, preferred_element_type=jnp.float32)
    return dot(ah, bh) + (dot(ah, bl) + dot(al, bh))


def band_kernel(flip, bases, offset, weight, high, low, full):
    count = bases.shape[0]
    extent = full.shape[0]
    width = extent // count
    step = min(width, 32)
    first = offset[0]
    for block in range(count):
        for row in range(0, width, step):
            place = lax.broadcasted_iota(jnp.int32, (step, extent), 0) + (bases[block] + row)
            gap = place - first
            value = jnp.zeros((step, extent), jnp.float32)
            for number in range(BAND):
                value = jnp.where(gap == number, weight[number, 0], value)
            full[pl.ds(block * width + row, step), :] = value
    matrix = full[...]
    if flip:
        matrix = matrix.T
    high[0], low[0] = halves(matrix)


def band_pair(offset, weight, bases, flip):
    states, extent = offset.shape
    out = jax.ShapeDtypeStruct((states, extent, extent), jnp.bfloat16)
    spec = pl.BlockSpec((1, extent, extent), lambda e: (e, 0, 0))
    return pl.pallas_call(
        functools.partial(band_kernel, flip),
        grid=(states,),
        out_shape=(out, out),
        in_specs=[
            pl.BlockSpec(memory_space=pltpu.SMEM),
            pl.BlockSpec((1, 1, extent), lambda e: (e, 0, 0)),
            pl.BlockSpec((BAND, 1, 1, extent), lambda e: (0, e, 0, 0)),
        ],
        out_specs=(spec, spec),
        scratch_shapes=[pltpu.VMEM((extent, extent), jnp.float32)],
        compiler_params=params(),
        cost_estimate=HINT,
        name="band",
    )(bases, offset[:, None, :], weight[:, :, None, :])


def mix_kernel(base, left_product, pieces, places, mixing, below, here, above, high, low, *rest):
    outs, (slabs, xh, xl, sems) = rest[:pieces], rest[pieces:]
    e = pl.program_id(0)
    quad = slabs.shape[0] // 3

    def fetch(source, group):
        place = places[group]
        return [
            pltpu.make_async_copy(source.at[i] if place is None else source.at[place[0], place[1] + i], slabs.at[group * quad + i], sems.at[group * quad + i])
            for i in range(quad)
        ]

    copies = fetch(below, 0) + fetch(here, 1) + fetch(above, 2)

    @pl.when(e == 0)
    def _():
        for copy in copies:
            copy.start()
        for copy in copies[: SPAN - 1]:
            copy.wait()

    for number in range(quad):

        @pl.when(e == number)
        def _():
            copies[number + SPAN - 1].wait()

    rows = xh.shape[0]
    step = min(rows, 16 * 1024 // xh.shape[1])
    shares = [mixing[base + e, d] for d in range(SPAN)]

    def chunk(i, carry):
        at = pl.ds(pl.multiple_of(i * step, step), step)
        total = shares[0] * slabs[e, at, :]
        for d in range(1, SPAN):
            total = total + shares[d] * slabs[e + d, at, :]
        xh[at, :], xl[at, :] = halves(total)
        return carry

    lax.fori_loop(0, rows // step, chunk, 0, unroll=2 if rows // step % 2 == 0 else 1)
    if left_product:
        result = dot3(high[0], low[0], xh[...], xl[...])
        width = result.shape[0] // pieces
        for s in range(pieces):
            outs[s][0] = result[s * width : (s + 1) * width]
    else:
        result = dot3(xh[...], xl[...], high[0], low[0])
        width = result.shape[1] // pieces
        for s in range(pieces):
            outs[s][0] = result[:, s * width : (s + 1) * width]


def mixed_product(sources, mixing, pair, base, left_product, pieces, after=()):
    quad = REACH
    arrays = [source[0] if isinstance(source, tuple) else source for source in sources]
    places = [source[1:] if isinstance(source, tuple) else None for source in sources]
    rows, columns = arrays[0].shape[-2:]
    extent = pair[0].shape[1]
    shape = (rows // pieces, columns) if left_product else (rows, columns // pieces)
    matrix = pl.BlockSpec((1, extent, extent), lambda e: (base + e, 0, 0))
    return ordered_call(
        functools.partial(mix_kernel, base, left_product, pieces, places),
        after,
        grid=(quad,),
        out_shape=[jax.ShapeDtypeStruct((quad,) + shape, jnp.float32)] * pieces,
        in_specs=[pl.BlockSpec(memory_space=pltpu.SMEM)]
        + [pl.BlockSpec(memory_space=pl.ANY)] * 3
        + [matrix] * 2,
        out_specs=[pl.BlockSpec((1,) + shape, lambda e: (e, 0, 0))] * pieces,
        scratch_shapes=[
            pltpu.VMEM((3 * quad, rows, columns), jnp.float32),
            pltpu.VMEM((rows, columns), jnp.bfloat16),
            pltpu.VMEM((rows, columns), jnp.bfloat16),
            pltpu.SemaphoreType.DMA((3 * quad,)),
        ],
        cost_estimate=HINT,
        name="mix_band",
    )(mixing, *arrays, *pair)


def column_kernel(pieces, high, low, *rest):
    parts, flows, (out, xh, xl) = rest[:pieces], rest[pieces : 2 * pieces], rest[2 * pieces :]
    rows = parts[0].shape[1]
    for s in range(pieces):
        at = pl.ds(s * rows, rows)
        xh[at, :], xl[at, :] = halves(parts[s][0])
    result = dot3(high[0], low[0], xh[...], xl[...])
    for s in range(pieces):
        at = pl.ds(s * rows, rows)
        out[0, at, :] = flows[s][0] + DISCOUNT * result[s * rows : (s + 1) * rows]


def column_product(parts, flows, pair, base, after=()):
    pieces = len(parts)
    quad, rows, columns = parts[0].shape
    extent = pair[0].shape[1]
    matrix = pl.BlockSpec((1, extent, extent), lambda e: (base + e, 0, 0))
    piece = pl.BlockSpec((1, rows, columns), lambda e: (e, 0, 0))
    return ordered_call(
        functools.partial(column_kernel, pieces),
        after,
        grid=(quad,),
        out_shape=jax.ShapeDtypeStruct((quad, extent, columns), jnp.float32),
        in_specs=[matrix] * 2 + [piece] * (2 * pieces),
        out_specs=pl.BlockSpec((1, extent, columns), lambda e: (e, 0, 0)),
        scratch_shapes=[pltpu.VMEM((extent, columns), jnp.bfloat16)] * 2,
        cost_estimate=HINT,
        name="columns_band",
    )(*pair, *parts, *flows)


def row_product_of(parts, high, low):
    width = parts[0].shape[2]
    result = None
    for s, part in enumerate(parts):
        xh, xl = halves(part[0])
        at = pl.ds(s * width, width)
        term = dot3(xh, xl, high[0, at, :], low[0, at, :])
        result = term if result is None else result + term
    return result


def last_row_kernel(pieces, high, low, flow, *rest):
    parts, out = rest[:pieces], rest[-1]
    out[0, 0] = flow[0, 0] + DISCOUNT * row_product_of(parts, high, low)


def last_rows(parts, pair, base, utility, age, whole, after=()):
    pieces = len(parts)
    quad, rows, columns = parts[0].shape
    extent = pair[0].shape[1]
    matrix = pl.BlockSpec((1, extent, extent), lambda e: (base + e, 0, 0))
    piece = pl.BlockSpec((1, rows, columns), lambda e: (e, 0, 0))
    flow = pl.BlockSpec((1, 1, rows, extent), lambda e: (age, base + e, 0, 0))
    before = () if whole is None else (whole,)
    return ordered_call(
        functools.partial(last_row_kernel, pieces),
        after,
        grid=(quad,),
        out_shape=jax.ShapeDtypeStruct(utility.shape, jnp.float32),
        in_specs=[matrix] * 2 + [flow] + [piece] * pieces + [pl.BlockSpec(memory_space=pl.ANY)] * len(before),
        out_specs=flow,
        input_output_aliases={} if whole is None else {3 + pieces: 0},
        cost_estimate=HINT,
        name="last_rows",
    )(*pair, utility, *parts, *before)


def take_kernel(place, flow, out):
    out[0] = flow[0, 0]


def taken_columns(utility, age, base, block, columns, after=()):
    quad = REACH
    rows = utility.shape[2]
    if columns % 128:
        return lax.dynamic_slice_in_dim(utility[age, base : base + quad], block * columns, columns, axis=2)
    return pl.pallas_call(
        lambda place, flow, *rest: take_kernel(place, flow, rest[-1]),
        out_shape=jax.ShapeDtypeStruct((quad, rows, columns), jnp.float32),
        grid_spec=pltpu.PrefetchScalarGridSpec(
            num_scalar_prefetch=1,
            grid=(quad,),
            in_specs=[pl.BlockSpec((1, 1, rows, columns), lambda e, place: (age, base + e, 0, place[0]))]
            + [pl.BlockSpec(memory_space=pl.ANY)] * len(after),
            out_specs=pl.BlockSpec((1, rows, columns), lambda e, place: (e, 0, 0)),
        ),
        compiler_params=params(),
        cost_estimate=HINT,
        name="take",
    )(jnp.reshape(jnp.asarray(block, jnp.int32), (1,)), utility, *after)


def shifted(value, axis, by):
    count = lax.axis_size(axis)
    return lax.ppermute(value, axis, [(i, i + by) for i in range(count) if 0 <= i + by < count])


def exchanged(pieces, by=0):
    count, ages = lax.axis_size("asset"), lax.axis_size("age")
    return [
        piece
        if s == 0 and by == 0
        else lax.ppermute(
            piece,
            ("asset", "age"),
            [
                (a * ages + z, (a + s) % count * ages + z + by)
                for a in range(count)
                for z in range(ages)
                if 0 <= z + by < ages
            ],
        )
        for s, piece in enumerate(pieces)
    ]


def local(
    values,
    utility,
    earn_prob,
    support_start,
    liquid_offset,
    liquid_weight,
    illiquid_offset,
    illiquid_weight,
):
    count = lax.axis_size("asset")
    me = lax.axis_index("asset")
    states = values.shape[1]
    quad = REACH
    assert states == 2 * quad
    rows = values.shape[2]
    columns = values.shape[3] // count

    ahead = [(me + s) % count for s in range(count)]
    behind = [(me - s + count) % count for s in range(count)]

    def in_blocks(x, blocks, width):
        return jnp.concatenate(
            [lax.dynamic_slice_in_dim(x, block * width, width, axis=x.ndim - 1) for block in blocks], axis=-1
        )

    def starts(blocks, width):
        return jnp.stack([jnp.asarray(block * width, jnp.int32) for block in blocks])

    natural_columns = starts(range(count), columns)
    behind_columns = starts(behind, columns)
    behind_rows = starts(behind, rows)

    liquid_first = band_pair(
        in_blocks(liquid_offset, ahead, columns), in_blocks(liquid_weight, ahead, columns), natural_columns, False
    )
    illiquid_first = band_pair(
        in_blocks(illiquid_offset, behind, rows), in_blocks(illiquid_weight, behind, rows), behind_rows, True
    )
    if count == 2:
        illiquid_second = illiquid_first
    else:
        illiquid_second = band_pair(
            in_blocks(illiquid_offset, ahead, rows), in_blocks(illiquid_weight, ahead, rows), behind_rows, True
        )
    liquid_second = band_pair(liquid_offset, liquid_weight, behind_columns, False)

    shares = earn_prob / jnp.sum(earn_prob, axis=0, keepdims=True)
    own = lax.axis_index("earn") * states + jnp.arange(states, dtype=jnp.int32)
    slots = jnp.arange(SPAN, dtype=jnp.int32)
    mixing = jnp.zeros((states, SPAN), jnp.float32)
    for number in range(REACH + 1):
        slot = support_start + number - own + REACH
        mixing = mixing + jnp.where(slots[None, :] == slot[:, None], shares[number][:, None], 0.0)

    def first_half(age, by, after, between):
        left = shifted(values[age, quad:], "earn", 1)
        right = shifted(values[age, :quad], "earn", -1)
        head, tail = (values, age, 0), (values, age, quad)
        parts = [mixed_product((left, head, tail), mixing, liquid_first, 0, False, count, after)]
        parts.append(mixed_product((head, tail, right), mixing, liquid_first, quad, False, count, (parts[0][0],) + between))
        return parts[1][0], [exchanged(part, by) for part in parts]

    def flow_columns(age, i, after):
        away = [taken_columns(utility, age, i * quad, block, columns, after) for block in ahead[1:]]

        sent = exchanged([away[-1]] + away)[1:]

        def with_own(stays):
            return [taken_columns(utility, age, i * quad, me, columns, stays)] + sent

        return away[-1], sent[-1], with_own

    def middle(arrived, flows, i, after):
        return column_product(arrived[i], flows[i], illiquid_first, i * quad, after)

    def second_half(sides, i, after):
        return mixed_product(sides, mixing, illiquid_second, i * quad, True, count, after)

    first, came_0, own_a0 = flow_columns(0, 0, ())
    second, came_1, own_a1 = flow_columns(0, 1, (first,))
    done, arrived_a = first_half(1, 0, (came_0,), ())
    flow_a = (own_a0((done,)), own_a1((done,)))
    done, arrived_b = first_half(0, -1, (done, came_1), ())
    first, came_0, own_b0 = flow_columns(1, 0, (done,))
    second, came_1, own_b1 = flow_columns(1, 1, (first,))

    head_a = middle(arrived_a, flow_a, 0, (second,))
    right_a = shifted(head_a, "earn", -1)
    flow_b = (own_b0((head_a,)), own_b1((head_a,)))
    tail_a = middle(arrived_a, flow_a, 1, (flow_b[1][0], came_0, came_1, *arrived_b[0], *arrived_b[1]))
    left_a = shifted(tail_a, "earn", 1)
    tail_b = middle(arrived_b, flow_b, 1, (tail_a,))
    left_b = shifted(tail_b, "earn", 1)
    head_b = middle(arrived_b, flow_b, 0, (tail_b,))
    right_b = shifted(head_b, "earn", -1)

    parts = second_half((head_a, tail_a, right_a), 1, (head_b,))
    last_a1 = exchanged(parts, -1)
    parts = second_half((left_a, head_a, tail_a), 0, (parts[0],))
    last_a0 = exchanged(parts, -1)
    parts = second_half((left_b, head_b, tail_b), 0, (parts[0],))
    last_b0 = exchanged(parts)
    parts = second_half((head_b, tail_b, right_b), 1, (parts[0],))
    last_b1 = exchanged(parts)
    whole = last_rows(last_a1, liquid_second, quad, utility, 1, None, (parts[0],))
    whole = last_rows(last_a0, liquid_second, 0, utility, 1, whole)
    whole = last_rows(last_b0, liquid_second, 0, utility, 0, whole)
    return last_rows(last_b1, liquid_second, quad, utility, 0, whole)


def solution(mesh):
    return jax.shard_map(
        local,
        mesh=mesh,
        in_specs=(
            P("age", "earn", "asset", None),
            P("age", "earn", "asset", None),
            P(None, "earn"),
            P("earn"),
            P("earn", None),
            P(None, "earn", None),
            P("earn", None),
            P(None, "earn", None),
        ),
        out_specs=P("age", "earn", "asset", None),
        check_vma=False,
    )
```
